256 devices in a mesh: prompt: 16 (over z, core), resp: 16 (over x, y).
Axes of the slice: x: 4, y: 4, z: 8, core: 2. Of those that a mesh axis runs over, the one named last changes fastest.
Arguments:
- inputs: bfloat16 [256, 128, 16384], P(('prompt', 'resp')), parts along dimension 0, may hold values from -6 to 6
- cotangent: bfloat16 [256, 128, 16384], P(('prompt', 'resp')), parts along dimension 0, may hold values from -96 to 96
- b_proj: bfloat16 [256, 128, 2048], P(('prompt', 'resp')), parts along dimension 0, may hold values from -0.375 to 0.375
- c_proj: bfloat16 [256, 128, 2048], P(('prompt', 'resp')), parts along dimension 0, may hold values from -0.375 to 0.375
- dt_raw: float32 [256, 128, 256], P(('prompt', 'resp')), parts along dimension 0, may hold values from -6 to 6
- decay_rate: float32 [256], replicated, may hold values from 0.003 to 0.06
- state_codes: bfloat16 [4096, 64, 256], P(('prompt', 'resp')), parts along dimension 0, may hold values from -6 to 6
- state_scales: bfloat16 [4096, 64], P(('prompt', 'resp')), parts along dimension 0, may hold values from 0.25 to 2
- sign_bucket: int32 [256], P(('prompt', 'resp')), parts along dimension 0, may hold values from 0 to 1
- adv_scale: float32 [256], P(('prompt', 'resp')), parts along dimension 0, may hold values from 0.5 to 2
- lengths: int32 [256], P(('prompt', 'resp')), parts along dimension 0, may hold values from 64 to 128, as said below
Outputs:
- grad_state: float32 [4096, 64, 256], P(('prompt', 'resp')), parts along dimension 0
- grad_b: bfloat16 [256, 128, 2048], P(('prompt', 'resp')), parts along dimension 0
- grad_c: bfloat16 [256, 128, 2048], P(('prompt', 'resp')), parts along dimension 0
- grad_dt: float32 [256, 128, 256], P(('prompt', 'resp')), parts along dimension 0
The draws below stay inside these ranges and needn't reach their ends.
There are 16 independent parts, one for each index of `prompt`. The reference program is written for one: setup_inputs(seed, part) draws one part's arguments, and reference() takes and returns one part's arrays. A program takes and returns all parts, laid end to end along the dimension named above; an argument that names none is the same for every part. Nothing has to cross between parts.
Inputs may be any that keep to these rules, and one draw needn't show every extreme that they name: `lengths`: every response has at least 64 valid tokens; some response of each prompt has exactly 128.
All inputs are finite; a program needn't handle non-finite values.
Results may differ from the reference program's by a relative error of at most 0.001.
Values may be sent and summed in bfloat16 or wider, within the bound.
No kernel may reach another device: no remote copies, remote signals or barrier semaphores. Data moves between devices by JAX's collectives and lax.ppermute only.
A program may use at most 128 MiB of HBM per device.

```python
import math
import jax
import jax.numpy as jnp
from jax import lax

H = 256
P_SIZE = 64
N = 256
G = 8
TOK = 128
RESP = 16


def draw_lengths(key, part):
    key = jax.random.fold_in(key, 11)
    first_key, second_key = jax.random.split(key)
    values = jax.random.randint(first_key, (RESP,), TOK // 2, TOK + 1)
    chosen = jax.random.randint(second_key, (), 0, RESP)
    return jnp.where(jnp.arange(RESP) == chosen, TOK, values).astype(jnp.int32)


def with_ends(drawn, stream_key, least, largest):
    longest = drawn.shape.index(max(drawn.shape))
    spots = []
    for shift in (0, 1):
        where = [jax.random.randint(jax.random.fold_in(stream_key, axis), (), 0, length) for axis, length in enumerate(drawn.shape)]
        where[longest] = (where[longest] + shift) % drawn.shape[longest]
        spots.append(tuple(where))
    return drawn.at[spots[0]].set(least).at[spots[1]].set(largest)


def level_of(key, shape, pieces, least, largest):
    level = 1.0
    for position, blocks in pieces:
        draws = jax.random.uniform(jax.random.fold_in(jax.random.fold_in(key, 6), position), (blocks,), jnp.float32, least / len(pieces), largest / len(pieces))
        level = level * jnp.repeat(jnp.exp(draws), shape[position] // blocks).reshape((-1,) + (1,) * (len(shape) - 1 - position))
    return level


def gaussian(key, extent, deviation, most, pieces=(), held_as=jnp.bfloat16):
    array = deviation * jax.random.normal(key, extent, jnp.float32)
    if pieces:
        array = array * level_of(key, extent, pieces, -0.22, 0.18)
    return jnp.clip(array, -most, most).astype(held_as)


def setup_inputs(seed: int = 0, part: int = 0) -> dict:
    keys = jax.random.split(jax.random.key(seed), 12)
    part_keys = jax.random.split(jax.random.fold_in(keys[11], part), 12)
    return {
        "inputs": gaussian(part_keys[0], (RESP, TOK, H * P_SIZE), 1.0, 6.0, ((0, 16),)),
        "cotangent": gaussian(part_keys[1], (RESP, TOK, H * P_SIZE), 16.0, 96.0, ((0, 16),)),
        "b_proj": gaussian(part_keys[2], (RESP, TOK, G * N), N ** -0.5, 0.375, ((0, 16),)),
        "c_proj": gaussian(part_keys[3], (RESP, TOK, G * N), N ** -0.5, 0.375, ((0, 16),)),
        "dt_raw": gaussian(part_keys[4], (RESP, TOK, H), 1.0, 6.0, ((0, 16),), jnp.float32),
        "decay_rate": jnp.clip(jnp.exp(jax.random.uniform(keys[5], (H,), jnp.float32, math.log(0.003), math.log(0.06))), 0.003, 0.06),
        "state_codes": gaussian(part_keys[6], (H, P_SIZE, N), 1.0, 6.0, ((0, 16),)),
        "state_scales": jnp.clip(jnp.exp(math.log(2.0) - 2.0794415 * jax.random.uniform(part_keys[7], (H, P_SIZE), jnp.float32) ** level_of(part_keys[7], (H, P_SIZE), ((0, 16),), -0.2, 0.2)), 0.25, 2.0).astype(jnp.bfloat16),
        "sign_bucket": with_ends(jax.random.randint(part_keys[8], (RESP,), 0, 2), jax.random.fold_in(part_keys[8], 1), 0, 1).astype(jnp.int32),
        "adv_scale": jnp.clip(jnp.exp(math.log(2.0) - 1.3862944 * jax.random.uniform(part_keys[9], (RESP,), jnp.float32) ** level_of(part_keys[9], (RESP,), ((0, 16),), -0.2, 0.2)), 0.5, 2.0),
        "lengths": draw_lengths(jax.random.fold_in(jax.random.fold_in(keys[11], part), 71), part),
    }


def group_forward(group_x, scores, group_c, group_dt, group_rate, group_state):
    tok_rows = group_x.shape[0]
    head_count = group_dt.shape[1]
    step_size = jax.nn.softplus(group_dt)
    log_decay = jnp.cumsum(-step_size * group_rate[None, :], axis=0)
    decay_rows = log_decay.T
    decay_gap = decay_rows[:, :, None] - decay_rows[:, None, :]
    causal = jnp.arange(tok_rows, dtype=jnp.int32)[:, None] >= jnp.arange(tok_rows, dtype=jnp.int32)[None, :]
    attenuation = jnp.where(causal[None], jnp.exp(jnp.where(causal[None], decay_gap, 0.0)), 0.0)
    mixing = attenuation * scores[None] * step_size.T[:, None, :]
    head_x = group_x.reshape(tok_rows, head_count, -1)
    within = jnp.einsum('hts,shp->thp', mixing, head_x, precision=lax.Precision.HIGHEST)
    carried = jnp.exp(log_decay)[:, :, None] * jnp.einsum('tn,hpn->thp', group_c, group_state, precision=lax.Precision.HIGHEST)
    return (within + carried).reshape(tok_rows, -1)

def response_grads(x_rows, up_rows, b_rows, c_rows, dt_rows, rate, prefix_state, row_coef, with_state):
    state_dim = prefix_state.shape[2]
    head_dim = prefix_state.shape[1]
    group_count = b_rows.shape[1] // state_dim
    group_heads = rate.shape[0] // group_count
    group_width = group_heads * head_dim
    tok_rows = x_rows.shape[0]

    def one_group(group_idx):
        group_x = lax.dynamic_slice_in_dim(x_rows, group_idx * group_width, group_width, 1).astype(jnp.float32)
        group_dy = lax.dynamic_slice_in_dim(up_rows, group_idx * group_width, group_width, 1).astype(jnp.float32) * row_coef[:, None]
        b_half = lax.dynamic_slice_in_dim(b_rows, group_idx * state_dim, state_dim, 1)
        c_half = lax.dynamic_slice_in_dim(c_rows, group_idx * state_dim, state_dim, 1)
        group_b = b_half.astype(jnp.float32)
        group_c = c_half.astype(jnp.float32)
        scores = jnp.dot(c_half, b_half.T, preferred_element_type=jnp.float32)
        group_dt = lax.dynamic_slice_in_dim(dt_rows, group_idx * group_heads, group_heads, 1)
        group_rate = lax.dynamic_slice_in_dim(rate, group_idx * group_heads, group_heads, 0)
        group_state = lax.dynamic_slice_in_dim(prefix_state, group_idx * group_heads, group_heads, 0)
        if with_state:

            def forward(s_in, c_in, dt_in, state_in):
                return group_forward(group_x, s_in, c_in, dt_in, group_rate, state_in)
            result, pullback = jax.vjp(forward, scores, group_c, group_dt, group_state)
        else:

            def forward(s_in, c_in, dt_in):
                return group_forward(group_x, s_in, c_in, dt_in, group_rate, group_state)
            result, pullback = jax.vjp(forward, scores, group_c, group_dt)
        grads = pullback(group_dy)
        d_scores = grads[0]
        grad_b = jnp.dot(d_scores.T, group_c, precision=lax.Precision.HIGHEST)
        grad_c = jnp.dot(d_scores, group_b, precision=lax.Precision.HIGHEST) + grads[1]
        return (grad_b, grad_c) + tuple(grads[2:])
    results = lax.map(one_group, jnp.arange(group_count, dtype=jnp.int32))
    grad_b = results[0].transpose(1, 0, 2).reshape(tok_rows, -1)
    grad_c = results[1].transpose(1, 0, 2).reshape(tok_rows, -1)
    grad_dt = results[2].transpose(1, 0, 2).reshape(tok_rows, -1)
    if with_state:
        return (grad_b, grad_c, grad_dt, results[3].reshape(rate.shape[0], head_dim, state_dim))
    return (grad_b, grad_c, grad_dt)

def reference(inputs, cotangent, b_proj, c_proj, dt_raw, decay_rate, state_codes, state_scales, sign_bucket, adv_scale, lengths):
    prefix_state = state_codes.astype(jnp.float32) * state_scales.astype(jnp.float32)[:, :, None]
    positions = jnp.arange(TOK, dtype=jnp.int32)

    def per_response(resp_idx):
        sign_value = 2.0 * sign_bucket[resp_idx].astype(jnp.float32) - 1.0
        coefficient = sign_value * adv_scale[resp_idx] / lengths[resp_idx].astype(jnp.float32)
        row_coef = jnp.where(positions < lengths[resp_idx], coefficient, jnp.zeros((), jnp.float32))
        return response_grads(inputs[resp_idx], cotangent[resp_idx], b_proj[resp_idx], c_proj[resp_idx], dt_raw[resp_idx], decay_rate, prefix_state, row_coef, True)
    grad_b, grad_c, grad_dt, grad_parts = lax.map(per_response, jnp.arange(RESP, dtype=jnp.int32))
    return (lax.optimization_barrier(jnp.sum(grad_parts, axis=0)), grad_b.astype(jnp.bfloat16), grad_c.astype(jnp.bfloat16), grad_dt)
```

```python
import functools

import jax
import jax.numpy as jnp
from jax import lax
from jax.experimental import pallas as pl
from jax.experimental.pallas import tpu as pltpu
from jax.sharding import Mesh, PartitionSpec as P

F32 = jnp.float32
BF16 = jnp.bfloat16

TOK = 128
H = 256
PS = 64
N = 256
G = 8
ROW = 4
RH = H // ROW
OH = RH // ROW
CH = OH // 2
CW = CH * PS
OW = OH * PS
RW = RH * PS
PW = ROW * CW
PACK0 = PW + 2 * N + 2 * RH
MIB = 1024 * 1024


def dot(a, b):
    return lax.dot_general(a, b, (((1,), (0,)), ((), ())), preferred_element_type=F32)


def dot_nt(a, b):
    return lax.dot_general(a, b, (((1,), (1,)), ((), ())), preferred_element_type=F32)


def dot_tn(a, b):
    return lax.dot_general(a, b, (((0,), (0,)), ((), ())), preferred_element_type=F32)


def split2(a):
    hi = a.astype(BF16)
    lo = (a - hi.astype(F32)).astype(BF16)
    return hi, lo


def split3(a):
    hi = a.astype(BF16)
    rest = a - hi.astype(F32)
    mid = rest.astype(BF16)
    lo = (rest - mid.astype(F32)).astype(BF16)
    return hi, mid, lo


def iota(shape, dim):
    return lax.broadcasted_iota(jnp.int32, shape, dim)


def softplus(a):
    return jnp.maximum(a, 0.0) + jnp.log1p(jnp.exp(-jnp.abs(a)))


def prep_kernel(
    x_idx, sign, adv, length, dt_ref, rate_ref, scale_ref, cot_hbm, c_hbm, codes_hbm, *rest
):
    packs0, packs1 = rest[0:4], rest[4:8]
    stp, ep_ref, fp_ref, sc_ref, sems = rest[8:13]
    me = x_idx[0]
    copies = []

    def start(src, dst):
        copy = pltpu.make_async_copy(src, dst, sems.at[len(copies)])
        copy.start()
        copies.append(copy)

    start(codes_hbm, stp.at[pl.ds(0, OW)])
    for k in (2, 1, 3, 0):
        there = lax.rem(me + k, ROW)
        for j in range(ROW):
            at = pl.multiple_of(there * RW + j * OW, CW)
            start(cot_hbm.at[0, :, pl.ds(at, CW)], packs0[k].at[:, pl.ds(j * CW, CW)])
        at = pl.multiple_of(there * 2 * N, 2 * N)
        start(c_hbm.at[0, :, pl.ds(at, 2 * N)], packs0[k].at[:, pl.ds(PW, 2 * N)])
    for k in (2, 1, 3, 0):
        there = lax.rem(me + k, ROW)
        for j in range(ROW):
            at = pl.multiple_of(there * RW + j * OW + CW, CW)
            start(cot_hbm.at[0, :, pl.ds(at, CW)], packs1[k].at[:, pl.ds(j * CW, CW)])

    step = softplus(dt_ref[0])
    tri = (iota((TOK, TOK), 0) >= iota((TOK, TOK), 1)).astype(F32).astype(BF16)
    s_hi, s_mid, s_lo = split3(step)
    total = dot(tri, s_hi) + dot(tri, s_mid) + dot(tri, s_lo)
    log_decay = -rate_ref[...] * total
    weight = (2.0 * sign[0].astype(F32) - 1.0) * adv[0] / jnp.full((TOK, H), length[0], jnp.int32).astype(F32)
    weight = jnp.where(iota((TOK, H), 0) < length[0], weight, 0.0)
    e_hi, e_lo = split2(weight * jnp.exp(log_decay))
    f_hi, f_lo = split2(step * jnp.exp(-log_decay))
    for q in range(ROW):
        cols = slice(q * RH, (q + 1) * RH)
        ep_ref[q] = jnp.concatenate([e_hi[:, cols], e_lo[:, cols]], axis=1)
        fp_ref[q] = jnp.concatenate([f_hi[:, cols], f_lo[:, cols]], axis=1)

    scale = scale_ref[...].astype(F32)
    two = jnp.concatenate([scale, scale], axis=1)
    tiled = jnp.concatenate([two] * (OW // 128), axis=1)
    own = iota((OH, OW), 0) == iota((OH, OW), 1) // PS
    row = dot(jnp.ones((OH, OH), BF16), jnp.where(own, tiled, 0.0).astype(BF16))
    held = jnp.zeros((OH, N), F32)
    for q in range(OW // N):
        held = jnp.where(iota((OH, N), 0) == q, row[:, q * N : (q + 1) * N], held)
    sc_ref[...] = held.astype(BF16)
    start(sc_ref, stp.at[pl.ds(OW, OH)])
    for k in (2, 1, 3, 0):
        there = lax.rem(me + k, ROW)
        start(ep_ref.at[there], packs0[k].at[:, pl.ds(PW + 2 * N, 2 * RH)])
    for copy in copies:
        copy.wait()


def prep(x_idx, sign, adv, length, dt, rate, scales, cot, c, codes):
    any_spec = pl.BlockSpec(memory_space=pl.ANY)
    smem = pl.BlockSpec(memory_space=pltpu.SMEM)
    vmem = pl.BlockSpec(memory_space=pltpu.VMEM)
    outs = pl.pallas_call(
        prep_kernel,
        out_shape=[jax.ShapeDtypeStruct((TOK, PACK0), BF16)] * 4
        + [jax.ShapeDtypeStruct((TOK, PW), BF16)] * 4
        + [jax.ShapeDtypeStruct((OW + OH, N), BF16)]
        + [jax.ShapeDtypeStruct((ROW, TOK, 2 * RH), BF16)] * 2,
        in_specs=[smem] * 4 + [vmem] * 3 + [any_spec] * 3,
        out_specs=[any_spec] * 9 + [vmem] * 2,
        scratch_shapes=[pltpu.VMEM((OH, N), BF16), pltpu.SemaphoreType.DMA((48,))],
        compiler_params=pltpu.CompilerParams(vmem_limit_bytes=16 * MIB),
        name="prep",
    )(x_idx, sign, adv, length, dt, rate, scales, cot, c, codes)
    return outs[0:4], outs[4:8], outs[8], outs[9], outs[10]


def within_kernel(x_ref, cot_ref, b_ref, c_ref, ep_ref, fp_ref, gb_ref, gc_ref, q_ref, sr_ref, sel_ref):
    g = pl.program_id(0)
    width = H // G * PS

    @pl.when(g == 0)
    def _():
        for half in range(2):
            row = iota((2 * RH, width), 0)
            head = iota((2 * RH, width), 1) // PS + half * (H // G)
            hit = (row == head) | (row == head + RH)
            sel_ref[half] = jnp.where(hit, 1.0, 0.0).astype(BF16)

    parity = lax.rem(g, 2)
    sel = sel_ref[parity]
    wide = dot(jnp.concatenate([ep_ref[0], fp_ref[0]], axis=0), sel)
    dy = cot_ref[0].astype(F32) * wide[:TOK]
    xs = x_ref[0].astype(F32) * wide[TOK:]
    d_hi, d_lo = split2(dy)
    x_hi, x_lo = split2(xs)
    b, c = b_ref[0], c_ref[0]
    rows, cols = iota((TOK, TOK), 0), iota((TOK, TOK), 1)
    s_hi, s_lo = split2(jnp.where(rows >= cols, dot_nt(c, b), 0.0))
    t_hi, t_lo = split2(jnp.where(rows <= cols, dot_nt(b, c), 0.0))
    d_two = jnp.concatenate([d_hi, d_lo], axis=0)
    x_two = jnp.concatenate([x_hi, x_lo], axis=0)
    y = dot(jnp.concatenate([s_hi, s_hi], axis=1), x_two) + dot(s_lo, x_hi)
    z = dot(jnp.concatenate([t_hi, t_hi], axis=1), d_two) + dot(t_lo, d_hi)
    ds4 = dot_nt(d_two, x_two)
    ds = ds4[:TOK, :TOK] + ds4[:TOK, TOK:] + ds4[TOK:, :TOK] + ds4[TOK:, TOK:]
    ds = jnp.where(rows >= cols, ds, 0.0)
    gb_ref[0] = dot(
        jnp.concatenate(split2(ds.T), axis=1), jnp.concatenate([c, c], axis=0)
    ).astype(BF16)
    gc_ref[...] = dot(jnp.concatenate(split2(ds), axis=1), jnp.concatenate([b, b], axis=0))
    q_hi, q_lo = split2(dy * y)
    r_hi, r_lo = split2(xs * z)
    seg = dot_nt(jnp.concatenate([q_hi, q_lo, r_hi, r_lo], axis=0), sel)
    q = seg[:TOK] + seg[TOK : 2 * TOK]
    sr = seg[2 * TOK : 3 * TOK] + seg[3 * TOK :]

    @pl.when(parity == 0)
    def _():
        q_ref[0] = q
        sr_ref[0] = sr

    @pl.when(parity == 1)
    def _():
        q_ref[0] += q
        sr_ref[0] += sr


def within(x, cot, b, c, ep, fp):
    width = H // G * PS
    wide = pl.BlockSpec((1, TOK, width), lambda g: (0, 0, g))
    narrow = pl.BlockSpec((1, TOK, N), lambda g: (0, 0, g))
    pair = pl.BlockSpec((1, TOK, 2 * RH), lambda g: (g // 2, 0, 0))
    return pl.pallas_call(
        within_kernel,
        grid=(G,),
        out_shape=[
            jax.ShapeDtypeStruct((1, TOK, G * N), BF16),
            jax.ShapeDtypeStruct((TOK, G * N), F32),
            jax.ShapeDtypeStruct((ROW, TOK, 2 * RH), F32),
            jax.ShapeDtypeStruct((ROW, TOK, 2 * RH), F32),
        ],
        in_specs=[wide, wide, narrow, narrow, pair, pair],
        out_specs=[narrow, pl.BlockSpec((TOK, N), lambda g: (0, g)), pair, pair],
        scratch_shapes=[pltpu.VMEM((2, 2 * RH, width), BF16)],
        compiler_params=pltpu.CompilerParams(vmem_limit_bytes=40 * MIB),
        cost_estimate=pl.CostEstimate(
            flops=12_000_000_000, bytes_accessed=12 * MIB, transcendentals=0
        ),
        name="within",
    )(x, cot, b, c, ep, fp)


def owner_kernel(chunk, *refs):
    cots, cs, es = refs[0:4], refs[4:8], refs[8:12]
    codes_ref, sc_ref = refs[12:14]
    olds = refs[14:18] if chunk else None
    outs = refs[18:] if chunk else refs[14:]
    gs_ref, rets = outs[0], outs[1:5]
    j = pl.program_id(0)

    @pl.when(j == 0)
    def _():
        for k in range(ROW):
            rets[k][...] = olds[k][...] if chunk else jnp.zeros_like(rets[k])

    cot = jnp.concatenate([r[...] for r in cots], axis=0).astype(F32)
    c = jnp.concatenate([r[...] for r in cs], axis=0)
    e = jnp.concatenate([r[...] for r in es], axis=0)
    held = sc_ref[0].astype(F32)
    at = chunk * CW // N
    scale = jnp.concatenate([held[at : at + 1], held[at + 1 : at + 2]], axis=1)
    row = iota((2 * RH, CW), 0)
    head = iota((2 * RH, CW), 1) // PS + j * OH + chunk * CH
    hit = (row == head) | (row == head + RH)
    sel = jnp.where(hit, 1.0, 0.0).astype(BF16)
    sel_scaled = jnp.where(hit, jnp.broadcast_to(scale, hit.shape), 0.0).astype(BF16)
    dy = cot * dot(e, sel_scaled)
    d_hi, d_lo = split2(dy)
    codes = codes_ref[0]
    gs_ref[0] = dot_tn(c, d_hi) + dot_tn(c, d_lo)
    gc = dot(d_hi, codes) + dot(d_lo, codes)
    p_hi, p_lo = split2(dy * dot_nt(c, codes))
    q = dot_nt(p_hi, sel) + dot_nt(p_lo, sel)
    for k in range(ROW):
        rets[k][:, 2 * N :] += q[k * TOK : (k + 1) * TOK]

    @pl.when(j < ROW // 2)
    def _():
        for k in range(ROW):
            rets[k][:, :N] += gc[k * TOK : (k + 1) * TOK]

    @pl.when(j >= ROW // 2)
    def _():
        for k in range(ROW):
            rets[k][:, N : 2 * N] += gc[k * TOK : (k + 1) * TOK]


def owner(chunk, cots, packs0, states, olds):
    cot_spec = pl.BlockSpec((TOK, CW), lambda j: (0, j))
    c_spec = pl.BlockSpec((TOK, N), lambda j: (0, PW // N + j // 2))
    e_spec = pl.BlockSpec((TOK, 2 * RH), lambda j: (0, (PW + 2 * N) // (2 * RH)))
    ret_spec = pl.BlockSpec((TOK, 2 * N + 2 * RH), lambda j: (0, 0))
    ret_shape = jax.ShapeDtypeStruct((TOK, 2 * N + 2 * RH), F32)
    outs = pl.pallas_call(
        functools.partial(owner_kernel, chunk),
        grid=(ROW,),
        out_shape=[jax.ShapeDtypeStruct((ROW, N, CW), F32)] + [ret_shape] * 4,
        in_specs=[cot_spec] * 4
        + [c_spec] * 4
        + [e_spec] * 4
        + [
            pl.BlockSpec((1, CW, N), lambda j: (j, chunk, 0)),
            pl.BlockSpec((1, OH, N), lambda j: (j, OW // OH, 0)),
        ]
        + [ret_spec] * (4 if chunk else 0),
        out_specs=[pl.BlockSpec((1, N, CW), lambda j: (j, 0, 0))] + [ret_spec] * 4,
        compiler_params=pltpu.CompilerParams(vmem_limit_bytes=40 * MIB),
        cost_estimate=pl.CostEstimate(
            flops=4_000_000_000, bytes_accessed=8 * MIB, transcendentals=0
        ),
        name=f"owner{chunk}",
    )(*cots, *packs0, *packs0, states, states, *(olds if chunk else ()))
    return outs[0], outs[1:]


def tokens_kernel(x_idx, dt_ref, rate_ref, gc_ref, q_ref, sr_ref, r0, r1, r2, r3, out_gc, out_dt):
    me = x_idx[0]
    lane = iota((TOK, H), 1) // RH
    q = jnp.zeros((TOK, H), F32)
    for k, ret in enumerate((r0, r1, r2, r3)):
        there = lax.rem(me + k, ROW)
        cols = pl.ds(pl.multiple_of(there * 2 * N, 2 * N), 2 * N)
        out_gc[0, :, cols] = (gc_ref[:, cols] + ret[:, : 2 * N]).astype(BF16)
        held = ret[:, 2 * N :]
        q = jnp.where(lane == there, jnp.concatenate([held, held], axis=1), q)
    sr = jnp.zeros((TOK, H), F32)
    for b in range(ROW):
        q = q + jnp.where(lane == b, jnp.concatenate([q_ref[b]] * 2, axis=1), 0.0)
        sr = sr + jnp.where(lane == b, jnp.concatenate([sr_ref[b]] * 2, axis=1), 0.0)
    dt = dt_ref[0]
    step = softplus(dt)
    tri = (iota((TOK, TOK), 0) <= iota((TOK, TOK), 1)).astype(F32).astype(BF16)
    a_hi, a_mid, a_lo = split3(q - sr)
    tail = dot(tri, a_hi) + dot(tri, a_mid) + dot(tri, a_lo)
    d_step = sr / step - rate_ref[...] * tail
    out_dt[0] = d_step / (1.0 + jnp.exp(-dt))


def tokens(x_idx, dt, rate, gc, q, sr, rets):
    smem = pl.BlockSpec(memory_space=pltpu.SMEM)
    vmem = pl.BlockSpec(memory_space=pltpu.VMEM)
    return pl.pallas_call(
        tokens_kernel,
        out_shape=[
            jax.ShapeDtypeStruct((1, TOK, G * N), BF16),
            jax.ShapeDtypeStruct((1, TOK, H), F32),
        ],
        in_specs=[smem] + [vmem] * 9,
        out_specs=[vmem] * 2,
        compiler_params=pltpu.CompilerParams(vmem_limit_bytes=24 * MIB),
        name="tokens",
    )(x_idx, dt, rate, gc, q, sr, *rets)


def state_kernel(a_ref, b_ref, sc_ref, out_ref):
    held = sc_ref[...].astype(F32)
    for chunk, ref in enumerate((a_ref, b_ref)):
        at = chunk * CW // N
        scale = jnp.concatenate([held[at : at + 1], held[at + 1 : at + 2]], axis=1)
        out_ref[pl.ds(chunk * CW, CW), :] = (ref[0] / scale).T


def state_out(a, b, stp):
    block = pl.BlockSpec((1, N, CW), lambda i: (0, 0, 0))
    return pl.pallas_call(
        state_kernel,
        grid=(1,),
        out_shape=jax.ShapeDtypeStruct((OW, N), F32),
        in_specs=[block, block, pl.BlockSpec((OH, N), lambda i: (OW // OH, 0))],
        out_specs=pl.BlockSpec((OW, N), lambda i: (0, 0)),
        compiler_params=pltpu.CompilerParams(vmem_limit_bytes=16 * MIB),
        name="state_out",
    )(a, b, stp)


def shift(k):
    return [(i, (i + k) % ROW) for i in range(ROW)]


def per_device(
    inputs, cotangent, b_proj, c_proj, dt_raw, decay_rate, state_codes, state_scales, sign, adv, lengths
):
    x_idx = lax.axis_index("rx").astype(jnp.int32)[None]
    rate = decay_rate[None]
    packs0, packs1, stp, ep, fp = prep(
        x_idx, sign, adv, lengths, dt_raw, rate, state_scales, cotangent, c_proj,
        state_codes.reshape(OW, N),
    )
    states = lax.all_gather(stp[None], "ry", axis=0, tiled=True)

    def exchange(packs):
        return [packs[0]] + [lax.ppermute(packs[k], "rx", shift(k)) for k in (1, 2, 3)]

    got0 = exchange(packs0)
    got1 = exchange(packs1)
    grad_b, gc_part, q, sr = within(inputs, cotangent, b_proj, c_proj, ep, fp)
    gs0, rets0 = owner(0, got0, got0, states, None)
    red0 = lax.psum_scatter(gs0, "ry", scatter_dimension=0, tiled=True)
    gs1, rets1 = owner(1, got1, got0, states, rets0)
    red1 = lax.psum_scatter(gs1, "ry", scatter_dimension=0, tiled=True)
    back = [rets1[0]] + [lax.ppermute(rets1[k], "rx", shift(-k)) for k in (1, 2, 3)]
    grad_c, grad_dt = tokens(x_idx, dt_raw, rate, gc_part, q, sr, back)
    grad_state = state_out(red0, red1, stp)
    return grad_state.reshape(OH, PS, N), grad_b, grad_c, grad_dt


def solution(mesh):
    prompts = mesh.shape["prompt"]
    mesh3 = Mesh(mesh.devices.reshape(prompts, ROW, ROW), ("prompt", "rx", "ry"))
    split = ("prompt", "rx", "ry")
    three = P(split, None, None)
    return jax.shard_map(
        per_device,
        mesh=mesh3,
        in_specs=(three,) * 5 + (P(), three, P(split, None)) + (P(split),) * 3,
        out_specs=(three,) * 4,
        check_vma=False,
    )
```

```python
import functools

import jax
import jax.numpy as jnp
from jax import lax
from jax.experimental import pallas as pl
from jax.experimental.pallas import tpu as pltpu
from jax.sharding import Mesh, PartitionSpec as P

F32 = jnp.float32
BF16 = jnp.bfloat16

TOK = 128
H = 256
PS = 64
N = 256
G = 8
ROW = 4
RH = H // ROW
OH = RH // ROW
OW = OH * PS
RW = RH * PS
CHS = (8, 8)
CWS = (CHS[0] * PS, CHS[1] * PS)
ATS = (0, CWS[0])
PWS = (ROW * CWS[0], ROW * CWS[1])
PACK0 = PWS[0] + 2 * N + 2 * RH
PAD = 16
TOP = 32752.0
MIB = 1024 * 1024
VMEM = 28 * MIB
SMALL = pl.CostEstimate(flops=1000, bytes_accessed=1000, transcendentals=0)


def dot(a, b):
    return lax.dot_general(a, b, (((1,), (0,)), ((), ())), preferred_element_type=F32)


def dot_nt(a, b):
    return lax.dot_general(a, b, (((1,), (1,)), ((), ())), preferred_element_type=F32)


def dot_tn(a, b):
    return lax.dot_general(a, b, (((0,), (0,)), ((), ())), preferred_element_type=F32)


def split2(a):
    hi = a.astype(BF16)
    lo = (a - hi.astype(F32)).astype(BF16)
    return hi, lo


def split3(a):
    hi = a.astype(BF16)
    rest = a - hi.astype(F32)
    mid = rest.astype(BF16)
    lo = (rest - mid.astype(F32)).astype(BF16)
    return hi, mid, lo


def iota(shape, dim):
    return lax.broadcasted_iota(jnp.int32, shape, dim)


def scale_row(held, chunk):
    first = ATS[chunk] // N
    rows = [held[q : q + 1] for q in range(first, first + CWS[chunk] // N)]
    return jnp.concatenate(rows, axis=1)


def softplus(a):
    return jnp.maximum(a, 0.0) + jnp.log1p(jnp.exp(-jnp.abs(a)))


def in_hbm(*arrays):
    return [pltpu.with_memory_space_constraint(a, pltpu.HBM) for a in arrays]


def prep_kernel(
    x_idx, y_idx, sign, adv, length, dt_hbm, rate_hbm, scale_hbm, cot_hbm, c_hbm, codes_hbm, *rest
):
    packs0, packs1 = rest[0:4], rest[4:8]
    stp, ep_ref, fp_ref, dt_ref, rate_ref, scale_ref, cot_v, c_v, codes_v, sc_ref, sems = rest[8:19]
    me = x_idx[0]
    order = (2, 1, 3, 0)
    owners = [lax.rem(y_idx[0] + ROW - j, ROW) for j in range(ROW)]
    started = []

    def start(src, dst):
        copy = pltpu.make_async_copy(src, dst, sems.at[len(started)])
        copy.start()
        started.append(copy)
        return copy

    load_dt = start(dt_hbm, dt_ref)
    load_rate = start(rate_hbm, rate_ref)
    load_scale = start(scale_hbm, scale_ref)
    loads = {}
    for k in order:
        there = lax.rem(me + k, ROW)
        at = pl.multiple_of(there * RW, RW)
        loads[k] = start(cot_hbm.at[0, :, pl.ds(at, RW)], cot_v.at[k])
    load_c = start(c_hbm.at[0], c_v)
    load_codes = start(codes_hbm, codes_v)

    load_dt.wait()
    load_rate.wait()
    step = softplus(dt_ref[0])
    tri = (iota((TOK, TOK), 0) >= iota((TOK, TOK), 1)).astype(F32).astype(BF16)
    s_hi, s_mid, s_lo = split3(step)
    total = dot(tri, s_hi) + dot(tri, s_mid) + dot(tri, s_lo)
    log_decay = -rate_ref[...] * total
    weight = (2.0 * sign[0].astype(F32) - 1.0) * adv[0] / jnp.full((TOK, H), length[0], jnp.int32).astype(F32)
    weight = jnp.where(iota((TOK, H), 0) < length[0], weight, 0.0)
    e_hi, e_lo = split2(weight * jnp.exp(log_decay))
    f_hi, f_lo = split2(step * jnp.exp(-log_decay))
    for q in range(ROW):
        cols = slice(q * RH, (q + 1) * RH)
        ep_ref[q] = jnp.concatenate([e_hi[:, cols], e_lo[:, cols]], axis=1)
        fp_ref[q] = jnp.concatenate([f_hi[:, cols], f_lo[:, cols]], axis=1)

    stores = []
    load_c.wait()
    for k in order:
        there = lax.rem(me + k, ROW)
        at = pl.multiple_of(there * 2 * N, 2 * N)
        stores.append(start(c_v.at[:, pl.ds(at, 2 * N)], packs0[k].at[:, pl.ds(PWS[0], 2 * N)]))
        stores.append(start(ep_ref.at[there], packs0[k].at[:, pl.ds(PWS[0] + 2 * N, 2 * RH)]))
    for k in order:
        loads[k].wait()
        for chunk, packs in enumerate((packs0, packs1)):
            width = CWS[chunk]
            for j in range(ROW):
                at = pl.multiple_of(owners[j] * OW + ATS[chunk], N)
                stores.append(
                    start(
                        cot_v.at[k, :, pl.ds(at, width)],
                        packs[k].at[:, pl.ds(j * width, width)],
                    )
                )
    load_codes.wait()
    stores.append(start(codes_v, stp.at[pl.ds(0, OW)]))

    load_scale.wait()
    scale = scale_ref[...].astype(F32)
    two = jnp.concatenate([scale, scale], axis=1)
    tiled = jnp.concatenate([two] * (OW // 128), axis=1)
    own = iota((OH, OW), 0) == iota((OH, OW), 1) // PS
    row = dot(jnp.ones((OH, OH), BF16), jnp.where(own, tiled, 0.0).astype(BF16))
    held = jnp.zeros((OH, N), F32)
    for q in range(OW // N):
        held = jnp.where(iota((OH, N), 0) == q, row[:, q * N : (q + 1) * N], held)
    sc_ref[...] = held.astype(BF16)
    stores.append(start(sc_ref, stp.at[pl.ds(OW, OH)]))
    for copy in stores:
        copy.wait()


def prep(x_idx, y_idx, sign, adv, length, dt, rate, scales, cot, c, codes):
    any_spec = pl.BlockSpec(memory_space=pl.ANY)
    hbm_spec = pl.BlockSpec(memory_space=pltpu.HBM)
    smem = pl.BlockSpec(memory_space=pltpu.SMEM)
    vmem = pl.BlockSpec(memory_space=pltpu.VMEM)
    outs = pl.pallas_call(
        prep_kernel,
        out_shape=[jax.ShapeDtypeStruct((TOK, PACK0), BF16)] * 4
        + [jax.ShapeDtypeStruct((TOK, PWS[1]), BF16)] * 4
        + [jax.ShapeDtypeStruct((OW + OH, N), BF16)]
        + [jax.ShapeDtypeStruct((ROW, TOK, 2 * RH), BF16)] * 2,
        in_specs=[smem] * 5 + [hbm_spec] * 6,
        out_specs=[any_spec] * 9 + [vmem] * 2,
        scratch_shapes=[
            pltpu.VMEM((1, TOK, H), F32),
            pltpu.VMEM((1, H), F32),
            pltpu.VMEM((OH, PS), BF16),
            pltpu.VMEM((ROW, TOK, RW), BF16),
            pltpu.VMEM((TOK, G * N), BF16),
            pltpu.VMEM((OW, N), BF16),
            pltpu.VMEM((OH, N), BF16),
            pltpu.SemaphoreType.DMA((64,)),
        ],
        compiler_params=pltpu.CompilerParams(vmem_limit_bytes=VMEM),
        cost_estimate=SMALL,
        name="prep",
    )(x_idx, y_idx, sign, adv, length, *in_hbm(dt, rate, scales, cot, c, codes))
    return outs[0:4], outs[4:8], outs[8], outs[9], outs[10]


def within_kernel(first, x_ref, cot_ref, b_ref, c_ref, ep_ref, fp_ref, *refs):
    gb_ref, gc_ref, q_ref, sr_ref, sel_ref = refs[-5:]
    g = pl.program_id(0) + first
    width = H // G * PS

    @pl.when(g == first)
    def _():
        for half in range(2):
            row = iota((2 * RH, width), 0)
            head = iota((2 * RH, width), 1) // PS + half * (H // G)
            hit = (row == head) | (row == head + RH)
            sel_ref[half] = jnp.where(hit, 1.0, 0.0).astype(BF16)

    parity = lax.rem(g, 2)
    sel = sel_ref[parity]
    wide = dot(jnp.concatenate([ep_ref[0], fp_ref[0]], axis=0), sel)
    dy = cot_ref[0].astype(F32) * wide[:TOK]
    xs = x_ref[0].astype(F32) * wide[TOK:]
    d_hi, d_lo = split2(dy)
    x_hi, x_lo = split2(xs)
    b, c = b_ref[0], c_ref[0]
    rows, cols = iota((TOK, TOK), 0), iota((TOK, TOK), 1)
    s_hi, s_lo = split2(jnp.where(rows >= cols, dot_nt(c, b), 0.0))
    t_hi, t_lo = split2(jnp.where(rows <= cols, dot_nt(b, c), 0.0))
    d_two = jnp.concatenate([d_hi, d_lo], axis=0)
    x_two = jnp.concatenate([x_hi, x_lo], axis=0)
    y = dot(jnp.concatenate([s_hi, s_hi], axis=1), x_two) + dot(s_lo, x_hi)
    z = dot(jnp.concatenate([t_hi, t_hi], axis=1), d_two) + dot(t_lo, d_hi)
    ds4 = dot_nt(d_two, x_two)
    ds = ds4[:TOK, :TOK] + ds4[:TOK, TOK:] + ds4[TOK:, :TOK] + ds4[TOK:, TOK:]
    ds = jnp.where(rows >= cols, ds, 0.0)
    gb_ref[0] = dot(
        jnp.concatenate(split2(ds.T), axis=1), jnp.concatenate([c, c], axis=0)
    ).astype(BF16)
    gc_ref[...] = dot(jnp.concatenate(split2(ds), axis=1), jnp.concatenate([b, b], axis=0))
    q_hi, q_lo = split2(dy * y)
    r_hi, r_lo = split2(xs * z)
    seg = dot_nt(jnp.concatenate([q_hi, q_lo, r_hi, r_lo], axis=0), sel)
    q = seg[:TOK] + seg[TOK : 2 * TOK]
    sr = seg[2 * TOK : 3 * TOK] + seg[3 * TOK :]

    @pl.when(parity == 0)
    def _():
        q_ref[0] = q
        sr_ref[0] = sr

    @pl.when(parity == 1)
    def _():
        q_ref[0] += q
        sr_ref[0] += sr


def within(first, last, x, cot, b, c, ep, fp, done):
    width = H // G * PS
    wide = pl.BlockSpec((1, TOK, width), lambda g: (0, 0, g + first))
    narrow = pl.BlockSpec((1, TOK, N), lambda g: (0, 0, g + first))
    pair = pl.BlockSpec((1, TOK, 2 * RH), lambda g: ((g + first) // 2, 0, 0))
    return pl.pallas_call(
        functools.partial(within_kernel, first),
        grid=(last - first,),
        out_shape=[
            jax.ShapeDtypeStruct((1, TOK, G * N), BF16),
            jax.ShapeDtypeStruct((TOK, G * N), F32),
            jax.ShapeDtypeStruct((ROW, TOK, 2 * RH), F32),
            jax.ShapeDtypeStruct((ROW, TOK, 2 * RH), F32),
        ],
        in_specs=[wide, wide, narrow, narrow, pair, pair]
        + [pl.BlockSpec(memory_space=pl.ANY)] * len(done),
        out_specs=[narrow, pl.BlockSpec((TOK, N), lambda g: (0, g + first)), pair, pair],
        scratch_shapes=[pltpu.VMEM((2, 2 * RH, width), BF16)],
        input_output_aliases={6 + i: i for i in range(len(done))},
        compiler_params=pltpu.CompilerParams(vmem_limit_bytes=VMEM),
        cost_estimate=SMALL,
        name=f"within{first}",
    )(*in_hbm(x, cot, b, c), ep, fp, *done)


def owner_kernel(chunk, y_idx, *refs):
    cots, cs, es = refs[0:4], refs[4:8], refs[8:12]
    codes_refs, sc_refs = refs[12:16], refs[16:20]
    olds = refs[20:24] if chunk else None
    outs = refs[24:] if chunk else refs[20:]
    own_ref, sends, rets = outs[0], outs[1:4], outs[4:8]
    me = y_idx[0]
    width = CWS[chunk]
    for r in range(ROW):
        rets[r][...] = olds[r][...] if chunk else jnp.zeros_like(rets[r])
    e = jnp.concatenate([r[...] for r in es], axis=0)
    for k in (2, 1, 3, 0):
        j = lax.rem(me + ROW - k, ROW)
        half = pl.ds(pl.multiple_of(j // 2 * N, N), N)
        cot = jnp.concatenate([r[:, k * width : (k + 1) * width] for r in cots], axis=0).astype(F32)
        c = jnp.concatenate([r[:, half] for r in cs], axis=0)
        held = sc_refs[k][...].astype(F32)
        scale = scale_row(held, chunk)
        row = iota((2 * RH, width), 0)
        head = iota((2 * RH, width), 1) // PS + j * OH + ATS[chunk] // PS
        hit = (row == head) | (row == head + RH)
        sel = jnp.where(hit, 1.0, 0.0).astype(BF16)
        sel_scaled = jnp.where(hit, jnp.broadcast_to(scale, hit.shape), 0.0).astype(BF16)
        dy = cot * dot(e, sel_scaled)
        d_hi, d_lo = split2(dy)
        codes = codes_refs[k][...]
        gs = dot_tn(c, d_hi) + dot_tn(c, d_lo)
        if k == 0:
            own_ref[...] = gs
        else:
            most = jnp.max(jnp.abs(gs), axis=0, keepdims=True)
            level = jnp.clip(jnp.ceil(jnp.log2(most) * 128.0), -14000.0, 14000.0)
            unit = TOP / jnp.exp2(level * (1.0 / 128.0))
            coded = jnp.round(gs * unit).astype(jnp.int32).astype(jnp.int16)
            sends[k - 1][:N] = coded
            sends[k - 1][N:] = jnp.broadcast_to(level.astype(jnp.int32), (PAD, width)).astype(jnp.int16)
        gc = dot(d_hi, codes) + dot(d_lo, codes)
        p_hi, p_lo = split2(dy * dot_nt(c, codes))
        q = dot_nt(p_hi, sel) + dot_nt(p_lo, sel)
        for r in range(ROW):
            rows = slice(r * TOK, (r + 1) * TOK)
            rets[r][:, half] += gc[rows]
            rets[r][:, 2 * N :] += q[rows]


def owner(chunk, y_idx, cots, packs0, states, olds):
    width = CWS[chunk]
    cot_spec = pl.BlockSpec((TOK, PWS[chunk]), lambda i: (0, 0))
    c_spec = pl.BlockSpec((TOK, 2 * N), lambda i: (0, PWS[0] // (2 * N)))
    e_spec = pl.BlockSpec((TOK, 2 * RH), lambda i: (0, (PWS[0] + 2 * N) // (2 * RH)))
    ret_spec = pl.BlockSpec((TOK, 2 * N + 2 * RH), lambda i: (0, 0))
    ret_shape = jax.ShapeDtypeStruct((TOK, 2 * N + 2 * RH), F32)
    send_spec = pl.BlockSpec((N + PAD, width), lambda i: (0, 0))
    outs = pl.pallas_call(
        functools.partial(owner_kernel, chunk),
        grid=(1,),
        out_shape=[jax.ShapeDtypeStruct((N, width), F32)]
        + [jax.ShapeDtypeStruct((N + PAD, width), jnp.int16)] * 3
        + [ret_shape] * 4,
        in_specs=[pl.BlockSpec(memory_space=pltpu.SMEM)]
        + [cot_spec] * 4
        + [c_spec] * 4
        + [e_spec] * 4
        + [pl.BlockSpec((width, N), lambda i: (ATS[chunk] // width, 0))] * 4
        + [pl.BlockSpec((OH, N), lambda i: (OW // OH, 0))] * 4
        + [ret_spec] * (4 if chunk else 0),
        out_specs=[pl.BlockSpec((N, width), lambda i: (0, 0))] + [send_spec] * 3 + [ret_spec] * 4,
        compiler_params=pltpu.CompilerParams(vmem_limit_bytes=VMEM),
        cost_estimate=SMALL,
        name=f"owner{chunk}",
    )(y_idx, *cots, *packs0, *packs0, *states, *states, *(olds if chunk else ()))
    return outs[0], list(outs[1:4]), list(outs[4:8])


def tokens_kernel(x_idx, dt_ref, rate_ref, gc_ref, q_ref, sr_ref, r0, r1, r2, r3, out_gc, out_dt):
    me = x_idx[0]
    lane = iota((TOK, H), 1) // RH
    q = jnp.zeros((TOK, H), F32)
    for k, ret in enumerate((r0, r1, r2, r3)):
        there = lax.rem(me + k, ROW)
        cols = pl.ds(pl.multiple_of(there * 2 * N, 2 * N), 2 * N)
        out_gc[0, :, cols] = (gc_ref[:, cols] + ret[:, : 2 * N]).astype(BF16)
        held = ret[:, 2 * N :]
        q = jnp.where(lane == there, jnp.concatenate([held, held], axis=1), q)
    sr = jnp.zeros((TOK, H), F32)
    for b in range(ROW):
        q = q + jnp.where(lane == b, jnp.concatenate([q_ref[b]] * 2, axis=1), 0.0)
        sr = sr + jnp.where(lane == b, jnp.concatenate([sr_ref[b]] * 2, axis=1), 0.0)
    dt = dt_ref[0]
    step = softplus(dt)
    tri = (iota((TOK, TOK), 0) <= iota((TOK, TOK), 1)).astype(F32).astype(BF16)
    a_hi, a_mid, a_lo = split3(q - sr)
    tail = dot(tri, a_hi) + dot(tri, a_mid) + dot(tri, a_lo)
    d_step = sr / step - rate_ref[...] * tail
    out_dt[0] = d_step / (1.0 + jnp.exp(-dt))


def tokens(x_idx, dt, rate, gc, q, sr, rets):
    smem = pl.BlockSpec(memory_space=pltpu.SMEM)
    vmem = pl.BlockSpec(memory_space=pltpu.VMEM)
    return pl.pallas_call(
        tokens_kernel,
        out_shape=[
            jax.ShapeDtypeStruct((1, TOK, G * N), BF16),
            jax.ShapeDtypeStruct((1, TOK, H), F32),
        ],
        in_specs=[smem] + [vmem] * 9,
        out_specs=[vmem] * 2,
        compiler_params=pltpu.CompilerParams(vmem_limit_bytes=VMEM),
        cost_estimate=SMALL,
        name="tokens",
    )(x_idx, dt, rate, gc, q, sr, *rets)


def state_kernel(*refs):
    sc_ref, out_ref = refs[8:10]
    held = sc_ref[...].astype(F32)
    for chunk in range(2):
        scale = scale_row(held, chunk)
        total = refs[4 * chunk][...]
        for ref in refs[4 * chunk + 1 : 4 * chunk + 4]:
            level = ref[N:].astype(jnp.int32).astype(F32)[:1]
            unit = jnp.exp2(level * (1.0 / 128.0)) * (1.0 / TOP)
            total = total + ref[:N].astype(jnp.int32).astype(F32) * unit
        out_ref[pl.ds(ATS[chunk], CWS[chunk]), :] = (total / scale).T


def state_out(own0, got0, own1, got1, stp):
    blocks = []
    for width in CWS:
        blocks += [pl.BlockSpec((N, width), lambda i: (0, 0))]
        blocks += [pl.BlockSpec((N + PAD, width), lambda i: (0, 0))] * 3
    return pl.pallas_call(
        state_kernel,
        grid=(1,),
        out_shape=jax.ShapeDtypeStruct((OW, N), F32),
        in_specs=blocks + [pl.BlockSpec((OH, N), lambda i: (OW // OH, 0))],
        out_specs=pl.BlockSpec((OW, N), lambda i: (0, 0)),
        compiler_params=pltpu.CompilerParams(vmem_limit_bytes=VMEM),
        cost_estimate=SMALL,
        name="state_out",
    )(own0, *got0, own1, *got1, stp)


def shift(k):
    return [(i, (i + k) % ROW) for i in range(ROW)]


def per_device(
    inputs, cotangent, b_proj, c_proj, dt_raw, decay_rate, state_codes, state_scales, sign, adv, lengths
):
    x_idx = lax.axis_index("rx").astype(jnp.int32)[None]
    y_idx = lax.axis_index("ry").astype(jnp.int32)[None]
    rate = decay_rate[None]
    packs0, packs1, stp, ep, fp = prep(
        x_idx, y_idx, sign, adv, lengths, dt_raw, rate, state_scales, cotangent, c_proj,
        state_codes.reshape(OW, N),
    )
    barrier = lax.optimization_barrier
    args = (inputs, cotangent, b_proj, c_proj, ep, fp)

    got0 = {k: lax.ppermute(packs0[k], "rx", shift(k)) for k in (2, 1, 3)}
    got0[0] = packs0[0]
    got0 = [got0[k] for k in range(ROW)]
    states = [stp, lax.ppermute(stp, "ry", shift(1)), None, lax.ppermute(stp, "ry", shift(3))]
    first = within(0, 4, *args, ())
    gc_part, state, states[1], states[3] = barrier((first[1], stp, states[1], states[3]))
    states[2] = lax.ppermute(state, "ry", shift(2))
    second = within(4, 6, *args, (first[0], gc_part, *first[2:]))
    gc_part, *send1 = barrier((second[1], *packs1[1:]))
    got1 = [packs1[0]] + [lax.ppermute(send1[k - 1], "rx", shift(k)) for k in (1, 2, 3)]
    gc_part, got0[0] = barrier((gc_part, got0[0]))
    own0, send0, rets0 = owner(0, y_idx, got0, got0, states, None)
    red0 = [None, lax.ppermute(send0[1], "ry", shift(-2)), lax.ppermute(send0[2], "ry", shift(-3))]
    gc_part, rets0[0] = barrier((gc_part, rets0[0]))
    grad_b, gc_part, q, sr = within(6, 8, *args, (second[0], gc_part, *second[2:]))
    gc_part, rets0[0], got1[0] = barrier((gc_part, rets0[0], got1[0]))
    last, *got1 = barrier((send0[0], *got1))
    red0[0] = lax.ppermute(last, "ry", shift(-1))
    red0[1], red0[2], got1[0] = barrier((red0[1], red0[2], got1[0]))
    own1, send1, rets1 = owner(1, y_idx, got1, got0, states, rets0)
    red0[0], a = barrier((red0[0], send1[0]))
    b, c = send1[1:]
    back = [rets1[0]] + [lax.ppermute(rets1[k], "rx", shift(-k)) for k in (1, 2, 3)]
    red1 = [lax.ppermute(send, "ry", shift(-k)) for k, send in ((1, a), (2, b), (3, c))]
    grad_c, grad_dt = tokens(x_idx, dt_raw, rate, gc_part, q, sr, back)
    grad_state = state_out(own0, red0, own1, red1, stp)
    return grad_state.reshape(OH, PS, N), grad_b, grad_c, grad_dt


def solution(mesh):
    prompts = mesh.shape["prompt"]
    mesh3 = Mesh(mesh.devices.reshape(prompts, ROW, ROW), ("prompt", "rx", "ry"))
    split = ("prompt", "rx", "ry")
    three = P(split, None, None)
    return jax.shard_map(
        per_device,
        mesh=mesh3,
        in_specs=(three,) * 5 + (P(), three, P(split, None)) + (P(split),) * 3,
        out_specs=(three,) * 4,
        check_vma=False,
    )
```

```python
import functools

import jax
import jax.numpy as jnp
from jax import lax
from jax.experimental import pallas as pl
from jax.experimental.pallas import tpu as pltpu
from jax.sharding import Mesh, PartitionSpec as P

F32 = jnp.float32
BF16 = jnp.bfloat16

TOK = 128
H = 256
PS = 64
N = 256
G = 8
ROW = 4
RH = H // ROW
OH = RH // ROW
OW = OH * PS
RW = RH * PS
CHS = (8, 8)
CWS = (CHS[0] * PS, CHS[1] * PS)
ATS = (0, CWS[0])
PWS = (ROW * CWS[0], ROW * CWS[1])
PACK0 = PWS[0] + 2 * N + 2 * RH
PAD = 16
TOP = 32752.0
MIB = 1024 * 1024
VMEM = 28 * MIB
SMALL = pl.CostEstimate(flops=1000, bytes_accessed=1000, transcendentals=0)


def dot(a, b):
    return lax.dot_general(a, b, (((1,), (0,)), ((), ())), preferred_element_type=F32)


def dot_nt(a, b):
    return lax.dot_general(a, b, (((1,), (1,)), ((), ())), preferred_element_type=F32)


def dot_tn(a, b):
    return lax.dot_general(a, b, (((0,), (0,)), ((), ())), preferred_element_type=F32)


def split2(a):
    hi = a.astype(BF16)
    lo = (a - hi.astype(F32)).astype(BF16)
    return hi, lo


def split3(a):
    hi = a.astype(BF16)
    rest = a - hi.astype(F32)
    mid = rest.astype(BF16)
    lo = (rest - mid.astype(F32)).astype(BF16)
    return hi, mid, lo


def iota(shape, dim):
    return lax.broadcasted_iota(jnp.int32, shape, dim)


def scale_row(held, chunk):
    first = ATS[chunk] // N
    rows = [held[q : q + 1] for q in range(first, first + CWS[chunk] // N)]
    return jnp.concatenate(rows, axis=1)


def softplus(a):
    return jnp.maximum(a, 0.0) + jnp.log1p(jnp.exp(-jnp.abs(a)))


def in_hbm(*arrays):
    return [pltpu.with_memory_space_constraint(a, pltpu.HBM) for a in arrays]


def prep_kernel(
    x_idx, y_idx, sign, adv, length, dt_hbm, rate_hbm, scale_hbm, cot_hbm, c_hbm, codes_hbm, *rest
):
    packs0, packs1 = rest[0:4], rest[4:8]
    stp, ep_ref, fp_ref, dt_ref, rate_ref, scale_ref, sc_ref, sems = rest[8:16]
    me = x_idx[0]
    order = (2, 1, 3, 0)
    owners = [lax.rem(y_idx[0] + ROW - j, ROW) for j in range(ROW)]
    started = []

    def start(src, dst):
        copy = pltpu.make_async_copy(src, dst, sems.at[len(started)])
        copy.start()
        started.append(copy)
        return copy

    load_dt = start(dt_hbm, dt_ref)
    load_rate = start(rate_hbm, rate_ref)
    load_scale = start(scale_hbm, scale_ref)
    stores = []
    for k in order:
        there = lax.rem(me + k, ROW)
        for chunk, packs in enumerate((packs0, packs1)):
            width = CWS[chunk]
            for j in range(ROW):
                at = pl.multiple_of(there * RW + owners[j] * OW + ATS[chunk], N)
                stores.append(
                    start(
                        cot_hbm.at[0, :, pl.ds(at, width)],
                        packs[k].at[:, pl.ds(j * width, width)],
                    )
                )
        at = pl.multiple_of(there * 2 * N, 2 * N)
        stores.append(start(c_hbm.at[0, :, pl.ds(at, 2 * N)], packs0[k].at[:, pl.ds(PWS[0], 2 * N)]))
    stores.append(start(codes_hbm, stp.at[pl.ds(0, OW)]))
    load_dt.wait()
    load_rate.wait()
    step = softplus(dt_ref[0])
    tri = (iota((TOK, TOK), 0) >= iota((TOK, TOK), 1)).astype(F32).astype(BF16)
    s_hi, s_mid, s_lo = split3(step)
    total = dot(tri, s_hi) + dot(tri, s_mid) + dot(tri, s_lo)
    log_decay = -rate_ref[...] * total
    weight = (2.0 * sign[0].astype(F32) - 1.0) * adv[0] / jnp.full((TOK, H), length[0], jnp.int32).astype(F32)
    weight = jnp.where(iota((TOK, H), 0) < length[0], weight, 0.0)
    e_hi, e_lo = split2(weight * jnp.exp(log_decay))
    f_hi, f_lo = split2(step * jnp.exp(-log_decay))
    for q in range(ROW):
        cols = slice(q * RH, (q + 1) * RH)
        ep_ref[q] = jnp.concatenate([e_hi[:, cols], e_lo[:, cols]], axis=1)
        fp_ref[q] = jnp.concatenate([f_hi[:, cols], f_lo[:, cols]], axis=1)

    for k in order:
        there = lax.rem(me + k, ROW)
        stores.append(start(ep_ref.at[there], packs0[k].at[:, pl.ds(PWS[0] + 2 * N, 2 * RH)]))

    load_scale.wait()
    scale = scale_ref[...].astype(F32)
    two = jnp.concatenate([scale, scale], axis=1)
    tiled = jnp.concatenate([two] * (OW // 128), axis=1)
    own = iota((OH, OW), 0) == iota((OH, OW), 1) // PS
    row = dot(jnp.ones((OH, OH), BF16), jnp.where(own, tiled, 0.0).astype(BF16))
    held = jnp.zeros((OH, N), F32)
    for q in range(OW // N):
        held = jnp.where(iota((OH, N), 0) == q, row[:, q * N : (q + 1) * N], held)
    sc_ref[...] = held.astype(BF16)
    stores.append(start(sc_ref, stp.at[pl.ds(OW, OH)]))
    for copy in stores:
        copy.wait()


def prep(x_idx, y_idx, sign, adv, length, dt, rate, scales, cot, c, codes):
    any_spec = pl.BlockSpec(memory_space=pl.ANY)
    hbm_spec = pl.BlockSpec(memory_space=pltpu.HBM)
    smem = pl.BlockSpec(memory_space=pltpu.SMEM)
    vmem = pl.BlockSpec(memory_space=pltpu.VMEM)
    outs = pl.pallas_call(
        prep_kernel,
        out_shape=[jax.ShapeDtypeStruct((TOK, PACK0), BF16)] * 4
        + [jax.ShapeDtypeStruct((TOK, PWS[1]), BF16)] * 4
        + [jax.ShapeDtypeStruct((OW + OH, N), BF16)]
        + [jax.ShapeDtypeStruct((ROW, TOK, 2 * RH), BF16)] * 2,
        in_specs=[smem] * 5 + [hbm_spec] * 6,
        out_specs=[any_spec] * 9 + [vmem] * 2,
        scratch_shapes=[
            pltpu.VMEM((1, TOK, H), F32),
            pltpu.VMEM((1, H), F32),
            pltpu.VMEM((OH, PS), BF16),
            pltpu.VMEM((OH, N), BF16),
            pltpu.SemaphoreType.DMA((64,)),
        ],
        compiler_params=pltpu.CompilerParams(vmem_limit_bytes=VMEM),
        cost_estimate=SMALL,
        name="prep",
    )(x_idx, y_idx, sign, adv, length, *in_hbm(dt, rate, scales, cot, c, codes))
    return outs[0:4], outs[4:8], outs[8], outs[9], outs[10]


def within_kernel(first, x_ref, cot_ref, b_ref, c_ref, ep_ref, fp_ref, *refs):
    gb_ref, gc_ref, q_ref, sr_ref, sel_ref = refs[-5:]
    g = pl.program_id(0) + first
    width = H // G * PS

    @pl.when(g == first)
    def _():
        for half in range(2):
            row = iota((2 * RH, width), 0)
            head = iota((2 * RH, width), 1) // PS + half * (H // G)
            hit = (row == head) | (row == head + RH)
            sel_ref[half] = jnp.where(hit, 1.0, 0.0).astype(BF16)

    parity = lax.rem(g, 2)
    sel = sel_ref[parity]
    wide = dot(jnp.concatenate([ep_ref[0], fp_ref[0]], axis=0), sel)
    dy = cot_ref[0].astype(F32) * wide[:TOK]
    xs = x_ref[0].astype(F32) * wide[TOK:]
    d_hi, d_lo = split2(dy)
    x_hi, x_lo = split2(xs)
    b, c = b_ref[0], c_ref[0]
    rows, cols = iota((TOK, TOK), 0), iota((TOK, TOK), 1)
    s_hi, s_lo = split2(jnp.where(rows >= cols, dot_nt(c, b), 0.0))
    t_hi, t_lo = split2(jnp.where(rows <= cols, dot_nt(b, c), 0.0))
    d_two = jnp.concatenate([d_hi, d_lo], axis=0)
    x_two = jnp.concatenate([x_hi, x_lo], axis=0)
    y = dot(jnp.concatenate([s_hi, s_hi], axis=1), x_two) + dot(s_lo, x_hi)
    z = dot(jnp.concatenate([t_hi, t_hi], axis=1), d_two) + dot(t_lo, d_hi)
    ds4 = dot_nt(d_two, x_two)
    ds = ds4[:TOK, :TOK] + ds4[:TOK, TOK:] + ds4[TOK:, :TOK] + ds4[TOK:, TOK:]
    ds = jnp.where(rows >= cols, ds, 0.0)
    gb_ref[0] = dot(
        jnp.concatenate(split2(ds.T), axis=1), jnp.concatenate([c, c], axis=0)
    ).astype(BF16)
    gc_ref[...] = dot(jnp.concatenate(split2(ds), axis=1), jnp.concatenate([b, b], axis=0))
    q_hi, q_lo = split2(dy * y)
    r_hi, r_lo = split2(xs * z)
    seg = dot_nt(jnp.concatenate([q_hi, q_lo, r_hi, r_lo], axis=0), sel)
    q = seg[:TOK] + seg[TOK : 2 * TOK]
    sr = seg[2 * TOK : 3 * TOK] + seg[3 * TOK :]

    @pl.when(parity == 0)
    def _():
        q_ref[0] = q
        sr_ref[0] = sr

    @pl.when(parity == 1)
    def _():
        q_ref[0] += q
        sr_ref[0] += sr


def within(first, last, x, cot, b, c, ep, fp, done):
    width = H // G * PS
    wide = pl.BlockSpec((1, TOK, width), lambda g: (0, 0, g + first))
    narrow = pl.BlockSpec((1, TOK, N), lambda g: (0, 0, g + first))
    pair = pl.BlockSpec((1, TOK, 2 * RH), lambda g: ((g + first) // 2, 0, 0))
    return pl.pallas_call(
        functools.partial(within_kernel, first),
        grid=(last - first,),
        out_shape=[
            jax.ShapeDtypeStruct((1, TOK, G * N), BF16),
            jax.ShapeDtypeStruct((TOK, G * N), F32),
            jax.ShapeDtypeStruct((ROW, TOK, 2 * RH), F32),
            jax.ShapeDtypeStruct((ROW, TOK, 2 * RH), F32),
        ],
        in_specs=[wide, wide, narrow, narrow, pair, pair]
        + [pl.BlockSpec(memory_space=pl.ANY)] * len(done),
        out_specs=[narrow, pl.BlockSpec((TOK, N), lambda g: (0, g + first)), pair, pair],
        scratch_shapes=[pltpu.VMEM((2, 2 * RH, width), BF16)],
        input_output_aliases={6 + i: i for i in range(len(done))},
        compiler_params=pltpu.CompilerParams(vmem_limit_bytes=VMEM),
        cost_estimate=SMALL,
        name=f"within{first}",
    )(*in_hbm(x, cot, b, c), ep, fp, *done)


def owner_kernel(chunk, y_idx, *refs):
    cots, cs, es = refs[0:4], refs[4:8], refs[8:12]
    codes_refs, sc_refs = refs[12:16], refs[16:20]
    olds = refs[20:24] if chunk else None
    outs = refs[24:] if chunk else refs[20:]
    own_ref, sends, rets = outs[0], outs[1:4], outs[4:8]
    me = y_idx[0]
    width = CWS[chunk]
    for r in range(ROW):
        rets[r][...] = olds[r][...] if chunk else jnp.zeros_like(rets[r])
    e = jnp.concatenate([r[...] for r in es], axis=0)
    for k in (2, 1, 3, 0):
        j = lax.rem(me + ROW - k, ROW)
        half = pl.ds(pl.multiple_of(j // 2 * N, N), N)
        cot = jnp.concatenate([r[:, k * width : (k + 1) * width] for r in cots], axis=0).astype(F32)
        c = jnp.concatenate([r[:, half] for r in cs], axis=0)
        held = sc_refs[k][...].astype(F32)
        scale = scale_row(held, chunk)
        row = iota((2 * RH, width), 0)
        head = iota((2 * RH, width), 1) // PS + j * OH + ATS[chunk] // PS
        hit = (row == head) | (row == head + RH)
        sel = jnp.where(hit, 1.0, 0.0).astype(BF16)
        sel_scaled = jnp.where(hit, jnp.broadcast_to(scale, hit.shape), 0.0).astype(BF16)
        dy = cot * dot(e, sel_scaled)
        d_hi, d_lo = split2(dy)
        codes = codes_refs[k][...]
        gs = dot_tn(c, d_hi) + dot_tn(c, d_lo)
        if k == 0:
            own_ref[...] = gs
        else:
            most = jnp.max(jnp.abs(gs), axis=0, keepdims=True)
            level = jnp.clip(jnp.ceil(jnp.log2(most) * 128.0), -14000.0, 14000.0)
            unit = TOP / jnp.exp2(level * (1.0 / 128.0))
            coded = jnp.round(gs * unit).astype(jnp.int32).astype(jnp.int16)
            sends[k - 1][:N] = coded
            sends[k - 1][N:] = jnp.broadcast_to(level.astype(jnp.int32), (PAD, width)).astype(jnp.int16)
        gc = dot(d_hi, codes) + dot(d_lo, codes)
        p_hi, p_lo = split2(dy * dot_nt(c, codes))
        q = dot_nt(p_hi, sel) + dot_nt(p_lo, sel)
        for r in range(ROW):
            rows = slice(r * TOK, (r + 1) * TOK)
            rets[r][:, half] += gc[rows]
            rets[r][:, 2 * N :] += q[rows]


def owner(chunk, y_idx, cots, packs0, states, olds):
    width = CWS[chunk]
    cot_spec = pl.BlockSpec((TOK, PWS[chunk]), lambda i: (0, 0))
    c_spec = pl.BlockSpec((TOK, 2 * N), lambda i: (0, PWS[0] // (2 * N)))
    e_spec = pl.BlockSpec((TOK, 2 * RH), lambda i: (0, (PWS[0] + 2 * N) // (2 * RH)))
    ret_spec = pl.BlockSpec((TOK, 2 * N + 2 * RH), lambda i: (0, 0))
    ret_shape = jax.ShapeDtypeStruct((TOK, 2 * N + 2 * RH), F32)
    send_spec = pl.BlockSpec((N + PAD, width), lambda i: (0, 0))
    outs = pl.pallas_call(
        functools.partial(owner_kernel, chunk),
        grid=(1,),
        out_shape=[jax.ShapeDtypeStruct((N, width), F32)]
        + [jax.ShapeDtypeStruct((N + PAD, width), jnp.int16)] * 3
        + [ret_shape] * 4,
        in_specs=[pl.BlockSpec(memory_space=pltpu.SMEM)]
        + [cot_spec] * 4
        + [c_spec] * 4
        + [e_spec] * 4
        + [pl.BlockSpec((width, N), lambda i: (ATS[chunk] // width, 0))] * 4
        + [pl.BlockSpec((OH, N), lambda i: (OW // OH, 0))] * 4
        + [ret_spec] * (4 if chunk else 0),
        out_specs=[pl.BlockSpec((N, width), lambda i: (0, 0))] + [send_spec] * 3 + [ret_spec] * 4,
        compiler_params=pltpu.CompilerParams(vmem_limit_bytes=VMEM),
        cost_estimate=SMALL,
        name=f"owner{chunk}",
    )(y_idx, *cots, *packs0, *packs0, *states, *states, *(olds if chunk else ()))
    return outs[0], list(outs[1:4]), list(outs[4:8])


def tokens_kernel(x_idx, dt_ref, rate_ref, gc_ref, q_ref, sr_ref, r0, r1, r2, r3, out_gc, out_dt):
    me = x_idx[0]
    lane = iota((TOK, H), 1) // RH
    q = jnp.zeros((TOK, H), F32)
    for k, ret in ((0, r0), (2, r1), (1, r2), (3, r3)):
        there = lax.rem(me + k, ROW)
        cols = pl.ds(pl.multiple_of(there * 2 * N, 2 * N), 2 * N)
        out_gc[0, :, cols] = (gc_ref[:, cols] + ret[:, : 2 * N]).astype(BF16)
        held = ret[:, 2 * N :]
        q = jnp.where(lane == there, jnp.concatenate([held, held], axis=1), q)
    sr = jnp.zeros((TOK, H), F32)
    for b in range(ROW):
        q = q + jnp.where(lane == b, jnp.concatenate([q_ref[b]] * 2, axis=1), 0.0)
        sr = sr + jnp.where(lane == b, jnp.concatenate([sr_ref[b]] * 2, axis=1), 0.0)
    dt = dt_ref[0]
    step = softplus(dt)
    tri = (iota((TOK, TOK), 0) <= iota((TOK, TOK), 1)).astype(F32).astype(BF16)
    a_hi, a_mid, a_lo = split3(q - sr)
    tail = dot(tri, a_hi) + dot(tri, a_mid) + dot(tri, a_lo)
    d_step = sr / step - rate_ref[...] * tail
    out_dt[0] = d_step / (1.0 + jnp.exp(-dt))


def tokens(x_idx, dt, rate, gc, q, sr, rets):
    smem = pl.BlockSpec(memory_space=pltpu.SMEM)
    vmem = pl.BlockSpec(memory_space=pltpu.VMEM)
    return pl.pallas_call(
        tokens_kernel,
        out_shape=[
            jax.ShapeDtypeStruct((1, TOK, G * N), BF16),
            jax.ShapeDtypeStruct((1, TOK, H), F32),
        ],
        in_specs=[smem] + [vmem] * 9,
        out_specs=[vmem] * 2,
        compiler_params=pltpu.CompilerParams(vmem_limit_bytes=VMEM),
        cost_estimate=SMALL,
        name="tokens",
    )(x_idx, dt, rate, gc, q, sr, *rets)


def state_kernel(*refs):
    sc_ref, out_ref = refs[8:10]
    held = sc_ref[...].astype(F32)
    for chunk in range(2):
        scale = scale_row(held, chunk)
        total = refs[4 * chunk][...]
        for ref in refs[4 * chunk + 1 : 4 * chunk + 4]:
            level = ref[N:].astype(jnp.int32).astype(F32)[:1]
            unit = jnp.exp2(level * (1.0 / 128.0)) * (1.0 / TOP)
            total = total + ref[:N].astype(jnp.int32).astype(F32) * unit
        out_ref[pl.ds(ATS[chunk], CWS[chunk]), :] = (total / scale).T


def state_out(own0, got0, own1, got1, stp):
    blocks = []
    for width in CWS:
        blocks += [pl.BlockSpec((N, width), lambda i: (0, 0))]
        blocks += [pl.BlockSpec((N + PAD, width), lambda i: (0, 0))] * 3
    return pl.pallas_call(
        state_kernel,
        grid=(1,),
        out_shape=jax.ShapeDtypeStruct((OW, N), F32),
        in_specs=blocks + [pl.BlockSpec((OH, N), lambda i: (OW // OH, 0))],
        out_specs=pl.BlockSpec((OW, N), lambda i: (0, 0)),
        compiler_params=pltpu.CompilerParams(vmem_limit_bytes=VMEM),
        cost_estimate=SMALL,
        name="state_out",
    )(own0, *got0, own1, *got1, stp)


def shift(k):
    return [(i, (i + k) % ROW) for i in range(ROW)]


def per_device(
    inputs, cotangent, b_proj, c_proj, dt_raw, decay_rate, state_codes, state_scales, sign, adv, lengths
):
    x_idx = lax.axis_index("rx").astype(jnp.int32)[None]
    y_idx = lax.axis_index("ry").astype(jnp.int32)[None]
    rate = decay_rate[None]
    packs0, packs1, stp, ep, fp = prep(
        x_idx, y_idx, sign, adv, lengths, dt_raw, rate, state_scales, cotangent, c_proj,
        state_codes.reshape(OW, N),
    )
    barrier = lax.optimization_barrier
    args = (inputs, cotangent, b_proj, c_proj, ep, fp)

    got0 = {k: lax.ppermute(packs0[k], "rx", shift(k)) for k in (2, 1, 3)}
    got0[0] = packs0[0]
    got0 = [got0[k] for k in range(ROW)]
    states = [stp, lax.ppermute(stp, "ry", shift(1)), None, lax.ppermute(stp, "ry", shift(3))]
    first = within(0, 4, *args, ())
    gc_part, state, states[1], states[3] = barrier((first[1], stp, states[1], states[3]))
    states[2] = lax.ppermute(state, "ry", shift(2))
    second = within(4, 6, *args, (first[0], gc_part, *first[2:]))
    gc_part, *send1 = barrier((second[1], *packs1[1:]))
    got1 = [packs1[0]] + [lax.ppermute(send1[k - 1], "rx", shift(k)) for k in (1, 2, 3)]
    gc_part, got0[0] = barrier((gc_part, got0[0]))
    own0, send0, rets0 = owner(0, y_idx, got0, got0, states, None)
    red0 = [None, lax.ppermute(send0[1], "ry", shift(-2)), lax.ppermute(send0[2], "ry", shift(-3))]
    gc_part, rets0[0] = barrier((gc_part, rets0[0]))
    grad_b, gc_part, q, sr = within(6, 8, *args, (second[0], gc_part, *second[2:]))
    gc_part, rets0[0], got1[0] = barrier((gc_part, rets0[0], got1[0]))
    last, *got1 = barrier((send0[0], *got1))
    red0[0] = lax.ppermute(last, "ry", shift(-1))
    red0[1], red0[2], got1[0] = barrier((red0[1], red0[2], got1[0]))
    own1, send1, rets1 = owner(1, y_idx, got1, got0, states, rets0)
    red0[0], *moved = barrier((red0[0], *rets1[1:], *send1))
    back = [rets1[0]] + [lax.ppermute(moved[k - 1], "rx", shift(-k)) for k in (2, 1, 3)]
    red1 = [lax.ppermute(moved[k + 2], "ry", shift(-k)) for k in (2, 1, 3)]
    grad_c, grad_dt = tokens(x_idx, dt_raw, rate, gc_part, q, sr, back)
    grad_dt, own1 = barrier((grad_dt, own1))
    grad_state = state_out(own0, red0, own1, red1, stp)
    return grad_state.reshape(OH, PS, N), grad_b, grad_c, grad_dt


def solution(mesh):
    prompts = mesh.shape["prompt"]
    mesh3 = Mesh(mesh.devices.reshape(prompts, ROW, ROW), ("prompt", "rx", "ry"))
    split = ("prompt", "rx", "ry")
    three = P(split, None, None)
    return jax.shard_map(
        per_device,
        mesh=mesh3,
        in_specs=(three,) * 5 + (P(), three, P(split, None)) + (P(split),) * 3,
        out_specs=(three,) * 4,
        check_vma=False,
    )
```

```python
import functools

import jax
import jax.numpy as jnp
from jax import lax
from jax.experimental import pallas as pl
from jax.experimental.pallas import tpu as pltpu
from jax.sharding import Mesh, PartitionSpec as P

F32 = jnp.float32
BF16 = jnp.bfloat16

TOK = 128
H = 256
PS = 64
N = 256
G = 8
ROW = 4
RH = H // ROW
OH = RH // ROW
OW = OH * PS
RW = RH * PS
CHS = (8, 8)
CWS = (CHS[0] * PS, CHS[1] * PS)
ATS = (0, CWS[0])
PWS = (ROW * CWS[0], ROW * CWS[1])
PACK0 = PWS[0] + 2 * N + 2 * RH
PAD = 16
TOP = 32752.0
MIB = 1024 * 1024
VMEM = 28 * MIB
SMALL = pl.CostEstimate(flops=1000, bytes_accessed=1000, transcendentals=0)


def dot(a, b):
    return lax.dot_general(a, b, (((1,), (0,)), ((), ())), preferred_element_type=F32)


def dot_nt(a, b):
    return lax.dot_general(a, b, (((1,), (1,)), ((), ())), preferred_element_type=F32)


def dot_tn(a, b):
    return lax.dot_general(a, b, (((0,), (0,)), ((), ())), preferred_element_type=F32)


def split2(a):
    hi = a.astype(BF16)
    lo = (a - hi.astype(F32)).astype(BF16)
    return hi, lo


def split3(a):
    hi = a.astype(BF16)
    rest = a - hi.astype(F32)
    mid = rest.astype(BF16)
    lo = (rest - mid.astype(F32)).astype(BF16)
    return hi, mid, lo


def iota(shape, dim):
    return lax.broadcasted_iota(jnp.int32, shape, dim)


def scale_row(held, chunk):
    first = ATS[chunk] // N
    rows = [held[q : q + 1] for q in range(first, first + CWS[chunk] // N)]
    return jnp.concatenate(rows, axis=1)


def softplus(a):
    return jnp.maximum(a, 0.0) + jnp.log1p(jnp.exp(-jnp.abs(a)))


def in_hbm(*arrays):
    return [pltpu.with_memory_space_constraint(a, pltpu.HBM) for a in arrays]


def prep_kernel(
    x_idx, y_idx, sign, adv, length, dt_hbm, rate_hbm, scale_hbm, cot_hbm, c_hbm, codes_hbm, *rest
):
    packs0, packs1 = rest[0:4], rest[4:8]
    stp, ep_ref, fp_ref, dt_ref, rate_ref, scale_ref, sc_ref, sems = rest[8:16]
    me = x_idx[0]
    order = (2, 1, 3, 0)
    owners = [lax.rem(y_idx[0] + ROW - j, ROW) for j in range(ROW)]
    started = []

    def start(src, dst):
        copy = pltpu.make_async_copy(src, dst, sems.at[len(started)])
        copy.start()
        started.append(copy)
        return copy

    load_dt = start(dt_hbm, dt_ref)
    load_rate = start(rate_hbm, rate_ref)
    load_scale = start(scale_hbm, scale_ref)
    stores = []
    for k in order:
        there = lax.rem(me + k, ROW)
        for chunk, packs in enumerate((packs0, packs1)):
            width = CWS[chunk]
            for j in range(ROW):
                at = pl.multiple_of(there * RW + owners[j] * OW + ATS[chunk], N)
                stores.append(
                    start(
                        cot_hbm.at[0, :, pl.ds(at, width)],
                        packs[k].at[:, pl.ds(j * width, width)],
                    )
                )
        at = pl.multiple_of(there * 2 * N, 2 * N)
        stores.append(start(c_hbm.at[0, :, pl.ds(at, 2 * N)], packs0[k].at[:, pl.ds(PWS[0], 2 * N)]))
    stores.append(start(codes_hbm, stp.at[pl.ds(0, OW)]))
    load_dt.wait()
    load_rate.wait()
    step = softplus(dt_ref[0])
    tri = (iota((TOK, TOK), 0) >= iota((TOK, TOK), 1)).astype(F32).astype(BF16)
    s_hi, s_mid, s_lo = split3(step)
    total = dot(tri, s_hi) + dot(tri, s_mid) + dot(tri, s_lo)
    log_decay = -rate_ref[...] * total
    weight = (2.0 * sign[0].astype(F32) - 1.0) * adv[0] / jnp.full((TOK, H), length[0], jnp.int32).astype(F32)
    weight = jnp.where(iota((TOK, H), 0) < length[0], weight, 0.0)
    e_hi, e_lo = split2(weight * jnp.exp(log_decay))
    f_hi, f_lo = split2(step * jnp.exp(-log_decay))
    for q in range(ROW):
        cols = slice(q * RH, (q + 1) * RH)
        ep_ref[q] = jnp.concatenate([e_hi[:, cols], e_lo[:, cols]], axis=1)
        fp_ref[q] = jnp.concatenate([f_hi[:, cols], f_lo[:, cols]], axis=1)

    for k in order:
        there = lax.rem(me + k, ROW)
        stores.append(start(ep_ref.at[there], packs0[k].at[:, pl.ds(PWS[0] + 2 * N, 2 * RH)]))

    load_scale.wait()
    scale = scale_ref[...].astype(F32)
    two = jnp.concatenate([scale, scale], axis=1)
    tiled = jnp.concatenate([two] * (OW // 128), axis=1)
    own = iota((OH, OW), 0) == iota((OH, OW), 1) // PS
    row = dot(jnp.ones((OH, OH), BF16), jnp.where(own, tiled, 0.0).astype(BF16))
    held = jnp.zeros((OH, N), F32)
    for q in range(OW // N):
        held = jnp.where(iota((OH, N), 0) == q, row[:, q * N : (q + 1) * N], held)
    sc_ref[...] = held.astype(BF16)
    stores.append(start(sc_ref, stp.at[pl.ds(OW, OH)]))
    for copy in stores:
        copy.wait()


def prep(x_idx, y_idx, sign, adv, length, dt, rate, scales, cot, c, codes):
    any_spec = pl.BlockSpec(memory_space=pl.ANY)
    hbm_spec = pl.BlockSpec(memory_space=pltpu.HBM)
    smem = pl.BlockSpec(memory_space=pltpu.SMEM)
    vmem = pl.BlockSpec(memory_space=pltpu.VMEM)
    outs = pl.pallas_call(
        prep_kernel,
        out_shape=[jax.ShapeDtypeStruct((TOK, PACK0), BF16)] * 4
        + [jax.ShapeDtypeStruct((TOK, PWS[1]), BF16)] * 4
        + [jax.ShapeDtypeStruct((OW + OH, N), BF16)]
        + [jax.ShapeDtypeStruct((ROW, TOK, 2 * RH), BF16)] * 2,
        in_specs=[smem] * 5 + [hbm_spec] * 6,
        out_specs=[any_spec] * 9 + [vmem] * 2,
        scratch_shapes=[
            pltpu.VMEM((1, TOK, H), F32),
            pltpu.VMEM((1, H), F32),
            pltpu.VMEM((OH, PS), BF16),
            pltpu.VMEM((OH, N), BF16),
            pltpu.SemaphoreType.DMA((64,)),
        ],
        compiler_params=pltpu.CompilerParams(vmem_limit_bytes=VMEM),
        cost_estimate=SMALL,
        name="prep",
    )(x_idx, y_idx, sign, adv, length, *in_hbm(dt, rate, scales, cot, c, codes))
    return outs[0:4], outs[4:8], outs[8], outs[9], outs[10]


def within_kernel(first, x_ref, cot_ref, b_ref, c_ref, ep_ref, fp_ref, *refs):
    gb_ref, gc_ref, q_ref, sr_ref, sel_ref = refs[-5:]
    g = pl.program_id(0) + first
    width = H // G * PS

    @pl.when(g == first)
    def _():
        for half in range(2):
            row = iota((2 * RH, width), 0)
            head = iota((2 * RH, width), 1) // PS + half * (H // G)
            hit = (row == head) | (row == head + RH)
            sel_ref[half] = jnp.where(hit, 1.0, 0.0).astype(BF16)

    parity = lax.rem(g, 2)
    sel = sel_ref[parity]
    wide = dot(jnp.concatenate([ep_ref[0], fp_ref[0]], axis=0), sel)
    dy = cot_ref[0].astype(F32) * wide[:TOK]
    xs = x_ref[0].astype(F32) * wide[TOK:]
    d_hi, d_lo = split2(dy)
    x_hi, x_lo = split2(xs)
    b, c = b_ref[0], c_ref[0]
    rows, cols = iota((TOK, TOK), 0), iota((TOK, TOK), 1)
    s_hi, s_lo = split2(jnp.where(rows >= cols, dot_nt(c, b), 0.0))
    t_hi, t_lo = split2(jnp.where(rows <= cols, dot_nt(b, c), 0.0))
    d_two = jnp.concatenate([d_hi, d_lo], axis=0)
    x_two = jnp.concatenate([x_hi, x_lo], axis=0)
    y = dot(jnp.concatenate([s_hi, s_hi], axis=1), x_two) + dot(s_lo, x_hi)
    z = dot(jnp.concatenate([t_hi, t_hi], axis=1), d_two) + dot(t_lo, d_hi)
    ds4 = dot_nt(d_two, x_two)
    ds = ds4[:TOK, :TOK] + ds4[:TOK, TOK:] + ds4[TOK:, :TOK] + ds4[TOK:, TOK:]
    ds = jnp.where(rows >= cols, ds, 0.0)
    gb_ref[0] = dot(
        jnp.concatenate(split2(ds.T), axis=1), jnp.concatenate([c, c], axis=0)
    ).astype(BF16)
    gc_ref[...] = dot(jnp.concatenate(split2(ds), axis=1), jnp.concatenate([b, b], axis=0))
    q_hi, q_lo = split2(dy * y)
    r_hi, r_lo = split2(xs * z)
    seg = dot_nt(jnp.concatenate([q_hi, q_lo, r_hi, r_lo], axis=0), sel)
    q = seg[:TOK] + seg[TOK : 2 * TOK]
    sr = seg[2 * TOK : 3 * TOK] + seg[3 * TOK :]

    @pl.when(parity == 0)
    def _():
        q_ref[0] = q
        sr_ref[0] = sr

    @pl.when(parity == 1)
    def _():
        q_ref[0] += q
        sr_ref[0] += sr


def within(first, last, x, cot, b, c, ep, fp, done):
    width = H // G * PS
    wide = pl.BlockSpec((1, TOK, width), lambda g: (0, 0, g + first))
    narrow = pl.BlockSpec((1, TOK, N), lambda g: (0, 0, g + first))
    pair = pl.BlockSpec((1, TOK, 2 * RH), lambda g: ((g + first) // 2, 0, 0))
    return pl.pallas_call(
        functools.partial(within_kernel, first),
        grid=(last - first,),
        out_shape=[
            jax.ShapeDtypeStruct((1, TOK, G * N), BF16),
            jax.ShapeDtypeStruct((TOK, G * N), F32),
            jax.ShapeDtypeStruct((ROW, TOK, 2 * RH), F32),
            jax.ShapeDtypeStruct((ROW, TOK, 2 * RH), F32),
        ],
        in_specs=[wide, wide, narrow, narrow, pair, pair]
        + [pl.BlockSpec(memory_space=pl.ANY)] * len(done),
        out_specs=[narrow, pl.BlockSpec((TOK, N), lambda g: (0, g + first)), pair, pair],
        scratch_shapes=[pltpu.VMEM((2, 2 * RH, width), BF16)],
        input_output_aliases={6 + i: i for i in range(len(done))},
        compiler_params=pltpu.CompilerParams(vmem_limit_bytes=VMEM),
        cost_estimate=SMALL,
        name=f"within{first}",
    )(*in_hbm(x, cot, b, c), ep, fp, *done)


def owner_kernel(chunk, y_idx, *refs):
    cots, cs, es = refs[0:4], refs[4:8], refs[8:12]
    codes_refs, sc_refs = refs[12:16], refs[16:20]
    olds = refs[20:24] if chunk else None
    outs = refs[24:] if chunk else refs[20:]
    own_ref, sends, rets = outs[0], outs[1:4], outs[4:8]
    me = y_idx[0]
    width = CWS[chunk]
    for r in range(ROW):
        rets[r][...] = olds[r][...] if chunk else jnp.zeros_like(rets[r])
    e = jnp.concatenate([r[...] for r in es], axis=0)
    for k in (2, 1, 3, 0):
        j = lax.rem(me + ROW - k, ROW)
        half = pl.ds(pl.multiple_of(j // 2 * N, N), N)
        cot = jnp.concatenate([r[:, k * width : (k + 1) * width] for r in cots], axis=0).astype(F32)
        c = jnp.concatenate([r[:, half] for r in cs], axis=0)
        held = sc_refs[k][...].astype(F32)
        scale = scale_row(held, chunk)
        row = iota((2 * RH, width), 0)
        head = iota((2 * RH, width), 1) // PS + j * OH + ATS[chunk] // PS
        hit = (row == head) | (row == head + RH)
        sel = jnp.where(hit, 1.0, 0.0).astype(BF16)
        sel_scaled = jnp.where(hit, jnp.broadcast_to(scale, hit.shape), 0.0).astype(BF16)
        dy = cot * dot(e, sel_scaled)
        d_hi, d_lo = split2(dy)
        codes = codes_refs[k][...]
        gs = dot_tn(c, d_hi) + dot_tn(c, d_lo)
        if k == 0:
            own_ref[...] = gs
        else:
            most = jnp.max(jnp.abs(gs), axis=0, keepdims=True)
            level = jnp.clip(jnp.ceil(jnp.log2(most) * 128.0), -14000.0, 14000.0)
            unit = TOP / jnp.exp2(level * (1.0 / 128.0))
            coded = jnp.round(gs * unit).astype(jnp.int32).astype(jnp.int16)
            sends[k - 1][:N] = coded
            sends[k - 1][N:] = jnp.broadcast_to(level.astype(jnp.int32), (PAD, width)).astype(jnp.int16)
        gc = dot(d_hi, codes) + dot(d_lo, codes)
        p_hi, p_lo = split2(dy * dot_nt(c, codes))
        q = dot_nt(sel, p_hi) + dot_nt(sel, p_lo)
        for r in range(ROW):
            rows = slice(r * TOK, (r + 1) * TOK)
            rets[r][:TOK, half] += gc[rows]
            for b in range(ROW):
                rets[r][TOK:, b * TOK : (b + 1) * TOK] += q[b * OH : (b + 1) * OH, rows]


def owner(chunk, y_idx, cots, packs0, states, olds):
    width = CWS[chunk]
    cot_spec = pl.BlockSpec((TOK, PWS[chunk]), lambda i: (0, 0))
    c_spec = pl.BlockSpec((TOK, 2 * N), lambda i: (0, PWS[0] // (2 * N)))
    e_spec = pl.BlockSpec((TOK, 2 * RH), lambda i: (0, (PWS[0] + 2 * N) // (2 * RH)))
    ret_spec = pl.BlockSpec((TOK + OH, 2 * N), lambda i: (0, 0))
    ret_shape = jax.ShapeDtypeStruct((TOK + OH, 2 * N), F32)
    send_spec = pl.BlockSpec((N + PAD, width), lambda i: (0, 0))
    outs = pl.pallas_call(
        functools.partial(owner_kernel, chunk),
        grid=(1,),
        out_shape=[jax.ShapeDtypeStruct((N, width), F32)]
        + [jax.ShapeDtypeStruct((N + PAD, width), jnp.int16)] * 3
        + [ret_shape] * 4,
        in_specs=[pl.BlockSpec(memory_space=pltpu.SMEM)]
        + [cot_spec] * 4
        + [c_spec] * 4
        + [e_spec] * 4
        + [pl.BlockSpec((width, N), lambda i: (ATS[chunk] // width, 0))] * 4
        + [pl.BlockSpec((OH, N), lambda i: (OW // OH, 0))] * 4
        + [ret_spec] * (4 if chunk else 0),
        out_specs=[pl.BlockSpec((N, width), lambda i: (0, 0))] + [send_spec] * 3 + [ret_spec] * 4,
        compiler_params=pltpu.CompilerParams(vmem_limit_bytes=VMEM),
        cost_estimate=SMALL,
        name=f"owner{chunk}",
    )(y_idx, *cots, *packs0, *packs0, *states, *states, *(olds if chunk else ()))
    return outs[0], list(outs[1:4]), list(outs[4:8])


def tokens_kernel(x_idx, dt_ref, rate_ref, gc_ref, q_ref, sr_ref, r0, r1, r2, r3, out_gc, out_dt):
    me = x_idx[0]
    lane = iota((TOK, H), 1) // RH
    q = jnp.zeros((TOK, H), F32)
    for k, ret in ((0, r0), (2, r1), (1, r2), (3, r3)):
        there = lax.rem(me + k, ROW)
        cols = pl.ds(pl.multiple_of(there * 2 * N, 2 * N), 2 * N)
        out_gc[0, :, cols] = (gc_ref[:, cols] + ret[:TOK]).astype(BF16)
        rows = [ret[TOK:, b * TOK : (b + 1) * TOK] for b in range(ROW)]
        held = jnp.concatenate(rows + rows, axis=0).T
        q = jnp.where(lane == there, jnp.concatenate([held, held], axis=1), q)
    sr = jnp.zeros((TOK, H), F32)
    for b in range(ROW):
        q = q + jnp.where(lane == b, jnp.concatenate([q_ref[b]] * 2, axis=1), 0.0)
        sr = sr + jnp.where(lane == b, jnp.concatenate([sr_ref[b]] * 2, axis=1), 0.0)
    dt = dt_ref[0]
    step = softplus(dt)
    tri = (iota((TOK, TOK), 0) <= iota((TOK, TOK), 1)).astype(F32).astype(BF16)
    a_hi, a_mid, a_lo = split3(q - sr)
    tail = dot(tri, a_hi) + dot(tri, a_mid) + dot(tri, a_lo)
    d_step = sr / step - rate_ref[...] * tail
    out_dt[0] = d_step / (1.0 + jnp.exp(-dt))


def tokens(x_idx, dt, rate, gc, q, sr, rets):
    smem = pl.BlockSpec(memory_space=pltpu.SMEM)
    vmem = pl.BlockSpec(memory_space=pltpu.VMEM)
    return pl.pallas_call(
        tokens_kernel,
        out_shape=[
            jax.ShapeDtypeStruct((1, TOK, G * N), BF16),
            jax.ShapeDtypeStruct((1, TOK, H), F32),
        ],
        in_specs=[smem] + [vmem] * 9,
        out_specs=[vmem] * 2,
        compiler_params=pltpu.CompilerParams(vmem_limit_bytes=VMEM),
        cost_estimate=SMALL,
        name="tokens",
    )(x_idx, dt, rate, gc, q, sr, *rets)


def state_kernel(*refs):
    sc_ref, out_ref = refs[8:10]
    held = sc_ref[...].astype(F32)
    for chunk in range(2):
        scale = scale_row(held, chunk)
        total = refs[4 * chunk][...]
        for ref in refs[4 * chunk + 1 : 4 * chunk + 4]:
            level = ref[N:].astype(jnp.int32).astype(F32)[:1]
            unit = jnp.exp2(level * (1.0 / 128.0)) * (1.0 / TOP)
            total = total + ref[:N].astype(jnp.int32).astype(F32) * unit
        out_ref[pl.ds(ATS[chunk], CWS[chunk]), :] = (total / scale).T


def state_out(own0, got0, own1, got1, stp):
    blocks = []
    for width in CWS:
        blocks += [pl.BlockSpec((N, width), lambda i: (0, 0))]
        blocks += [pl.BlockSpec((N + PAD, width), lambda i: (0, 0))] * 3
    return pl.pallas_call(
        state_kernel,
        grid=(1,),
        out_shape=jax.ShapeDtypeStruct((OW, N), F32),
        in_specs=blocks + [pl.BlockSpec((OH, N), lambda i: (OW // OH, 0))],
        out_specs=pl.BlockSpec((OW, N), lambda i: (0, 0)),
        compiler_params=pltpu.CompilerParams(vmem_limit_bytes=VMEM),
        cost_estimate=SMALL,
        name="state_out",
    )(own0, *got0, own1, *got1, stp)


def shift(k):
    return [(i, (i + k) % ROW) for i in range(ROW)]


def per_device(
    inputs, cotangent, b_proj, c_proj, dt_raw, decay_rate, state_codes, state_scales, sign, adv, lengths
):
    x_idx = lax.axis_index("rx").astype(jnp.int32)[None]
    y_idx = lax.axis_index("ry").astype(jnp.int32)[None]
    rate = decay_rate[None]
    packs0, packs1, stp, ep, fp = prep(
        x_idx, y_idx, sign, adv, lengths, dt_raw, rate, state_scales, cotangent, c_proj,
        state_codes.reshape(OW, N),
    )
    barrier = lax.optimization_barrier
    args = (inputs, cotangent, b_proj, c_proj, ep, fp)

    got0 = {k: lax.ppermute(packs0[k], "rx", shift(k)) for k in (2, 1, 3)}
    got0[0] = packs0[0]
    got0 = [got0[k] for k in range(ROW)]
    far = lax.ppermute(stp, "ry", shift(2))
    first = within(0, 4, *args, ())
    gc_part, state, far = barrier((first[1], stp, far))
    states = [stp, lax.ppermute(state, "ry", shift(1)), far, lax.ppermute(state, "ry", shift(3))]
    second = within(4, 6, *args, (first[0], gc_part, *first[2:]))
    gc_part, *send1 = barrier((second[1], *packs1[1:]))
    got1 = [packs1[0]] + [lax.ppermute(send1[k - 1], "rx", shift(k)) for k in (1, 2, 3)]
    gc_part, got0[0] = barrier((gc_part, got0[0]))
    own0, send0, rets0 = owner(0, y_idx, got0, got0, states, None)
    red0 = [None, lax.ppermute(send0[1], "ry", shift(-2)), lax.ppermute(send0[2], "ry", shift(-3))]
    gc_part, rets0[0] = barrier((gc_part, rets0[0]))
    grad_b, gc_part, q, sr = within(6, 8, *args, (second[0], gc_part, *second[2:]))
    gc_part, rets0[0], got1[0] = barrier((gc_part, rets0[0], got1[0]))
    last, *got1 = barrier((send0[0], *got1))
    red0[0] = lax.ppermute(last, "ry", shift(-1))
    red0[1], red0[2], got1[0] = barrier((red0[1], red0[2], got1[0]))
    own1, send1, rets1 = owner(1, y_idx, got1, got0, states, rets0)
    red0[0], *moved = barrier((red0[0], *rets1[1:], *send1))
    back = [rets1[0]] + [lax.ppermute(moved[k - 1], "rx", shift(-k)) for k in (2, 1, 3)]
    red1 = [lax.ppermute(moved[k + 2], "ry", shift(-k)) for k in (2, 1, 3)]
    grad_c, grad_dt = tokens(x_idx, dt_raw, rate, gc_part, q, sr, back)
    grad_dt, own1 = barrier((grad_dt, own1))
    grad_state = state_out(own0, red0, own1, red1, stp)
    return grad_state.reshape(OH, PS, N), grad_b, grad_c, grad_dt


def solution(mesh):
    prompts = mesh.shape["prompt"]
    mesh3 = Mesh(mesh.devices.reshape(prompts, ROW, ROW), ("prompt", "rx", "ry"))
    split = ("prompt", "rx", "ry")
    three = P(split, None, None)
    return jax.shard_map(
        per_device,
        mesh=mesh3,
        in_specs=(three,) * 5 + (P(), three, P(split, None)) + (P(split),) * 3,
        out_specs=(three,) * 4,
        check_vma=False,
    )
```
